32 devices in a mesh: row: 4 (over y, x), col: 8 (over z, core).
Axes of the slice: x: 2, y: 2, z: 4, core: 2. Of those that a mesh axis runs over, the one named last changes fastest.
Arguments:
- tokens: bfloat16 [1024, 8192], P('row', 'col'), may hold values from -6 to 6
- w_in: bfloat16 [8192, 3, 8192], P('row', None, 'col'), may hold values from -0.0625 to 0.0625
- filt_in: float32 [7, 3, 8192], P(None, None, 'col'), may hold values from -2.4 to 2.4
- filt_mix: float32 [7, 8192], P(None, 'col'), may hold values from -2.4 to 2.4
Outputs:
- gated: bfloat16 [1024, 8192], P('row', 'col')
The draws below stay inside these ranges and needn't reach their ends.
All inputs are finite; a program needn't handle non-finite values.
Results may differ from the reference program's by a relative error of at most 0.0064.
Values may be sent and summed in bfloat16 or wider, within the bound.
No kernel may reach another device: no remote copies, remote signals or barrier semaphores. Data moves between devices by JAX's collectives and lax.ppermute only.
A program may use at most 128 MiB of HBM per device.

```python
import jax
import jax.numpy as jnp

D = 8192
KERNEL = 7
TOKENS = 1024


def steps_of(rng, shape, cuts, smallest, top_value):
    level, own = 1.0, jax.random.fold_in(rng, 6)
    for axis_at, blocks in cuts:
        heights = jnp.exp(jax.random.uniform(jax.random.fold_in(own, axis_at), (blocks,), jnp.float32, smallest / len(cuts), top_value / len(cuts)))
        level = level * jnp.repeat(heights, shape[axis_at] // blocks).reshape([-1 if axis == axis_at else 1 for axis in range(len(shape))])
    return level


def bell_draw(rng, dims, scale, most, shards=(), dtype=jnp.bfloat16):
    gain = steps_of(rng, dims, shards, -0.22, 0.18) if shards else 1.0
    drawn = jax.random.normal(rng, dims, jnp.float32) * scale * gain
    return jnp.minimum(jnp.maximum(drawn, -most), most).astype(dtype)


def setup_inputs(seed: int = 0) -> dict:
    seeds = jax.random.split(jax.random.key(seed), 5)
    tokens = bell_draw(seeds[0], (TOKENS, D), 1.0, 6.0, ((0, 4), (1, 8)))
    w_in = bell_draw(seeds[1], (D, 3, D), D ** -0.5, 0.0625, ((0, 4), (2, 8)))
    filt_in = bell_draw(seeds[2], (KERNEL, 3, D), 0.4, 2.4, ((2, 8),), jnp.float32)
    filt_mix = bell_draw(seeds[3], (KERNEL, D), 0.4, 2.4, ((1, 8),), jnp.float32)
    return {"tokens": tokens, "w_in": w_in, "filt_in": filt_in, "filt_mix": filt_mix}


def taps(ext, filt, count):
    total = filt[0] * ext[6:6 + count]
    for shift_s in range(1, 7):
        total = total + filt[shift_s] * ext[6 - shift_s:6 - shift_s + count]
    return total


def reference(tokens, w_in, filt_in, filt_mix):
    flat = jnp.dot(tokens, w_in.reshape(D, 3 * D), preferred_element_type=jnp.float32)
    proj = flat.astype(jnp.bfloat16).reshape(TOKENS, 3, D).astype(jnp.float32)
    padded = jnp.pad(proj, ((6, 0), (0, 0), (0, 0)))
    conv = taps(padded, filt_in, TOKENS)
    prod = conv[:, 1] * conv[:, 2]
    padded_prod = jnp.pad(prod, ((6, 0), (0, 0)))
    mix = taps(padded_prod, filt_mix, TOKENS)
    return (conv[:, 0] * mix).astype(jnp.bfloat16)
```

```python
import jax
import jax.numpy as jnp
from jax import lax
from jax.sharding import PartitionSpec as P

CORES = 2
HALO = 12
CHUNKS = 2


def side(n):
    x = 1
    while x * x < n:
        x *= 2
    return n // x, x


def shift_rows(block, shape, dy, dx):
    ys, xs = shape
    route = []
    for y in range(ys):
        for x in range(xs):
            route.append((((y + dy) % ys) * xs + (x + dx) % xs, y * xs + x))
    return lax.ppermute(block, "row", route)


def taps(ext, filt, count):
    total = filt[0] * ext[6 : 6 + count]
    for shift_s in range(1, 7):
        total = total + filt[shift_s] * ext[6 - shift_s : 6 - shift_s + count]
    return total


def gather_tokens(piece, shape):
    ys, xs = shape
    cols = lax.axis_size("col")
    groups = [list(range(k, cols, CORES)) for k in range(CORES)]
    strip = lax.all_gather(piece, "col", axis=0, axis_index_groups=groups)
    me = lax.axis_index("row")
    y, x = me // xs, me % xs
    parts = []
    for dy in range(ys):
        for dx in range(xs):
            target = ((y - dy) % ys) * xs + (x - dx) % xs
            block = lax.dynamic_index_in_dim(strip, target, 0, keepdims=False)
            parts.append(block if dy == dx == 0 else shift_rows(block, shape, dy, dx))
    mine = jnp.stack(parts)
    swap = [(c, c ^ 1) for c in range(cols)]
    other = lax.ppermute(mine, "col", swap)
    first = lax.axis_index("col") % CORES == 0
    lo = jnp.where(first, mine, other)
    hi = jnp.where(first, other, mine)
    return jnp.concatenate([lo, hi], axis=2)


def mm(a, w):
    return jnp.dot(a, w, preferred_element_type=jnp.float32)


def project(blocks, w, shape):
    ys, xs = shape
    n = blocks.shape[1]
    m = w.shape[1]
    h = n // 2
    k = blocks.shape[2]
    b = blocks.reshape(ys, xs, n, k)
    a, c = b[:, :, :h], b[:, :, h:]
    sent_a = [mm(a[:, dx].reshape(ys * h, k), w).astype(jnp.bfloat16) for dx in range(1, xs)]
    sent_c = [mm(c[dy].reshape(xs * h, k), w).astype(jnp.bfloat16) for dy in range(1, ys)]
    got_a = [shift_rows(s, shape, 0, -dx) for dx, s in enumerate(sent_a, 1)]
    got_c = [shift_rows(s, shape, -dy, 0) for dy, s in enumerate(sent_c, 1)]
    sum_a = mm(a[:, 0].reshape(ys * h, k), w)
    sum_c = mm(c[0].reshape(xs * h, k), w)
    for g in got_a:
        sum_a = sum_a + g.astype(jnp.float32)
    for g in got_c:
        sum_c = sum_c + g.astype(jnp.float32)
    sum_a = sum_a.reshape(ys, h, m)
    sum_c = sum_c.reshape(xs, h, m)
    end_a, end_c = sum_a[0], sum_c[0]
    for dy in range(1, ys):
        end_a = end_a + shift_rows(sum_a[dy].astype(jnp.bfloat16), shape, -dy, 0).astype(jnp.float32)
    for dx in range(1, xs):
        end_c = end_c + shift_rows(sum_c[dx].astype(jnp.bfloat16), shape, 0, -dx).astype(jnp.float32)
    return jnp.concatenate([end_a, end_c], axis=0)


def per_device(tokens, w_in, filt_in, filt_mix):
    rows = tokens.shape[0]
    cols = w_in.shape[2]
    shape = side(lax.axis_size("row"))
    w = w_in.reshape(w_in.shape[0], 3 * cols)
    n = rows // CHUNKS
    done = []
    for q in reversed(range(CHUNKS)):
        blocks = gather_tokens(tokens[q * n : (q + 1) * n], shape)
        done.insert(0, project(blocks, w, shape))
    last = done[-1][n - HALO :].astype(jnp.bfloat16)
    count = lax.axis_size("row")
    rim = lax.ppermute(last, "row", [(i, i + 1) for i in range(count - 1)])
    proj = jnp.concatenate([rim.astype(jnp.float32)] + done, axis=0).reshape(rows + HALO, 3, cols)
    conv = taps(proj, filt_in, rows + 6)
    prod = conv[:, 1] * conv[:, 2]
    mix = taps(prod, filt_mix, rows)
    return (conv[6:, 0] * mix).astype(jnp.bfloat16)


def solution(mesh):
    return jax.shard_map(
        per_device,
        mesh=mesh,
        in_specs=(P("row", "col"), P("row", None, "col"), P(None, None, "col"), P(None, "col")),
        out_specs=P("row", "col"),
        check_vma=False,
    )
```

```python
import functools

import jax
import jax.numpy as jnp
from jax import lax
from jax.experimental import pallas as pl
from jax.experimental.pallas import tpu as pltpu
from jax.sharding import PartitionSpec as P

CORES = 2
RIM = 16
PARTS = 4
LANES = 128
VMEM = pl.BlockSpec(memory_space=pltpu.VMEM)
HBM = pl.BlockSpec(memory_space=pl.ANY)
BF16, F32 = jnp.bfloat16, jnp.float32


def params(mib=16):
    return pltpu.CompilerParams(vmem_limit_bytes=mib * 2**20)


def cost(flops, moved):
    return pl.CostEstimate(flops=flops, bytes_accessed=moved, transcendentals=0)


def side(n):
    x = 1
    while x * x < n:
        x *= 2
    return n // x, x


def shift_rows(block, shape, dy, dx):
    ys, xs = shape
    route = []
    for y in range(ys):
        for x in range(xs):
            route.append((((y + dy) % ys) * xs + (x + dx) % xs, y * xs + x))
    return lax.ppermute(block, "row", route)


def shift_planes(block, dz):
    cols = lax.axis_size("col")
    return lax.ppermute(block, "col", [((c + CORES * dz) % cols, c) for c in range(cols)])


def fetch_kernel(w_ref, o_ref, sem):
    half = o_ref.shape[2]
    core = lax.rem(lax.axis_index("col"), CORES)
    copies = []
    for g in range(3):
        for j in range(2):
            start = pl.multiple_of((core if j == 0 else 1 - core) * half, half)
            copies.append(pltpu.make_async_copy(w_ref.at[g, pl.ds(start, half)], o_ref.at[g, j], sem.at[2 * g + j]))
    for c in copies:
        c.start()
    for c in copies:
        c.wait()


def fetch(w_in):
    w = w_in.transpose(1, 0, 2)
    g, k, n = w.shape
    return pl.pallas_call(
        fetch_kernel,
        in_specs=[HBM],
        out_specs=VMEM,
        out_shape=pltpu.VMEM((g, 2, k // 2, n), BF16),
        scratch_shapes=[pltpu.SemaphoreType.DMA((2 * g,))],
        compiler_params=params(),
        name="fetch_w",
    )(w)


def pick_kernel(shape, *refs):
    ys, xs = shape
    zs = ys * xs
    ins, outs = refs[:zs], refs[zs:]
    me = lax.axis_index("row")
    y, x = me // xs, lax.rem(me, xs)
    z = lax.axis_index("col") // CORES
    for dy in range(ys):
        for dx in range(xs):
            target = lax.rem(y - dy + ys, ys) * xs + lax.rem(x - dx + xs, xs)
            want = lax.rem(target - z + zs, zs)
            for dz in range(zs):

                @pl.when(want == dz)
                def _():
                    outs[dy * xs + dx][...] = ins[dz][...]


def gather_tokens(piece, shape):
    ys, xs = shape
    zs = ys * xs
    strips = [piece] + [shift_planes(piece, dz) for dz in range(1, zs)]
    picked = pl.pallas_call(
        functools.partial(pick_kernel, shape),
        in_specs=[VMEM] * zs,
        out_specs=[VMEM] * zs,
        out_shape=[pltpu.VMEM(piece.shape, BF16)] * zs,
        compiler_params=params(),
        name="pick",
    )(*strips)
    return [picked[0]] + [shift_rows(picked[i], shape, i // xs, i % xs) for i in range(1, zs)]


def stack_kernel(order, *refs):
    ins, out = refs[:-1], refs[-1]
    h = ins[0].shape[0] // 2
    for at, (block, part) in enumerate(order):
        out[at * h : (at + 1) * h] = ins[block][part * h : (part + 1) * h]


def stack(blocks, shape):
    ys, xs = shape
    order = [(dy * xs + dx, 0) for dx in range(1, xs) for dy in range(ys)]
    order += [(dy * xs + dx, 1) for dy in range(1, ys) for dx in range(xs)]
    order += [(dy * xs, 0) for dy in range(ys)] + [(dx, 1) for dx in range(xs)]
    n, e = blocks[0].shape
    return pl.pallas_call(
        functools.partial(stack_kernel, order),
        in_specs=[VMEM] * len(blocks),
        out_specs=VMEM,
        out_shape=pltpu.VMEM((len(blocks) * n, e), BF16),
        compiler_params=params(),
        name="stack",
    )(*blocks)


def project_kernel(tn, mine, other, w_ref, *outs):
    n = w_ref.shape[3]
    for g in range(3):
        for j in range(n // tn):
            cols = slice(j * tn, (j + 1) * tn)
            acc = jnp.dot(mine[...], w_ref[g, 0, :, cols], preferred_element_type=F32)
            acc = acc + jnp.dot(other[...], w_ref[g, 1, :, cols], preferred_element_type=F32)
            at = 0
            for o in outs:
                o[:, g * n + j * tn : g * n + (j + 1) * tn] = acc[at : at + o.shape[0]].astype(o.dtype)
                at += o.shape[0]


def project(mine, other, w, h, shape):
    ys, xs = shape
    m, e = mine.shape
    cols = w.shape[3]
    sizes = [(ys * h, BF16)] * (xs - 1) + [(xs * h, BF16)] * (ys - 1) + [(ys * h, F32), (xs * h, F32)]
    outs = pl.pallas_call(
        functools.partial(project_kernel, min(cols, 256)),
        in_specs=[VMEM] * 3,
        out_specs=[VMEM] * len(sizes),
        out_shape=[pltpu.VMEM((s, 3 * cols), t) for s, t in sizes],
        compiler_params=params(),
        cost_estimate=cost(2 * m * 2 * e * 3 * cols, 2 * w.size),
        name="project",
    )(mine, other, w)
    return outs[: xs - 1], outs[xs - 1 : xs + ys - 2], outs[-2], outs[-1]


def middle_kernel(count_a, count_c, *refs):
    keep_a, got_a = refs[0], refs[1 : 1 + count_a]
    keep_c, got_c = refs[1 + count_a], refs[2 + count_a : 2 + count_a + count_c]
    outs = refs[2 + count_a + count_c :]
    h = outs[0].shape[0]
    for keep, got, mids in ((keep_a, got_a, outs[:count_c]), (keep_c, got_c, outs[count_c:])):
        for i, mid in enumerate(mids, 1):
            total = keep[i * h : (i + 1) * h]
            for g in got:
                total = total + g[i * h : (i + 1) * h].astype(F32)
            mid[...] = total.astype(BF16)


def exchange(outs, h, shape):
    ys, xs = shape
    sent_a, sent_c, keep_a, keep_c = outs
    got_a = [shift_rows(s, shape, 0, -dx) for dx, s in enumerate(sent_a, 1)]
    got_c = [shift_rows(s, shape, -dy, 0) for dy, s in enumerate(sent_c, 1)]
    n = keep_a.shape[1]
    mids = pl.pallas_call(
        functools.partial(middle_kernel, xs - 1, ys - 1),
        in_specs=[VMEM] * (2 + xs - 1 + ys - 1),
        out_specs=[VMEM] * (xs + ys - 2),
        out_shape=[pltpu.VMEM((h, n), BF16)] * (xs + ys - 2),
        compiler_params=params(),
        name="middle",
    )(keep_a, *got_a, keep_c, *got_c)
    last_a = [shift_rows(s, shape, -dy, 0) for dy, s in enumerate(mids[: ys - 1], 1)]
    last_c = [shift_rows(s, shape, 0, -dx) for dx, s in enumerate(mids[ys - 1 :], 1)]
    return [keep_a, *got_a, *last_a], [keep_c, *got_c, *last_c]


def finish_kernel(q, parts, n, count_a, count_c, *refs):
    refs = list(refs)
    terms = [refs[:count_a], refs[count_a : count_a + count_c]]
    del refs[: count_a + count_c]
    fin, fmix = refs.pop(0), refs.pop(0)
    follow = refs.pop(0) if q < parts - 1 else None
    rim = refs.pop(0) if q == 0 else None
    out = refs.pop(0)
    lead = refs.pop(0) if q > 0 else None
    tail = refs.pop(0) if q == parts - 1 else None
    ext, prod = refs
    h = n // 2
    for i, group in enumerate(terms):
        total = group[0][:h]
        for g in group[1:]:
            total = total + g[:h].astype(F32)
        ext[RIM + i * h : RIM + (i + 1) * h] = total
    if follow is not None:
        ext[RIM + n : RIM + n + RIM] = follow[...]
    if rim is not None:
        ext[:RIM] = rim[...].astype(F32)
    if lead is not None:
        lead[...] = ext[RIM : 2 * RIM]
    if tail is not None:
        tail[...] = ext[n : n + RIM].astype(BF16)
    cols = fmix.shape[1]
    first = RIM if q == 0 else 2 * RIM
    rows = out.shape[0]
    step = 48 if rows % 48 == 0 else (40 if rows % 40 == 0 else 16)
    step = min(step, rows)
    if rows % 64 == 0:
        step = 64

    def column(c, _):
        at = pl.multiple_of(c * LANES, LANES)

        def conv(g, start, count):
            where = pl.ds(pl.multiple_of(g * cols + at, LANES), LANES)
            total = fin[g, 0:1, pl.ds(at, LANES)] * ext[start : start + count, where]
            for s in range(1, 7):
                total = total + fin[g, s : s + 1, pl.ds(at, LANES)] * ext[start - s : start - s + count, where]
            return total

        for r in range(0, rows, step):
            base = first + r
            prod[: step + 8] = conv(1, base - 8, step + 8) * conv(2, base - 8, step + 8)
            mix = fmix[0:1, pl.ds(at, LANES)] * prod[8 : 8 + step]
            for s in range(1, 7):
                mix = mix + fmix[s : s + 1, pl.ds(at, LANES)] * prod[8 - s : 8 - s + step]
            out[r : r + step, pl.ds(at, LANES)] = (conv(0, base, step) * mix).astype(BF16)
        return 0

    lax.fori_loop(0, cols // LANES, column, 0)


def finish(q, parts, n, terms_a, terms_c, fin, fmix, follow, rim):
    width = terms_a[0].shape[1]
    cols = fmix.shape[1]
    rows = n + (RIM if q == 0 else 0) - (RIM if q == parts - 1 else 0)
    args = [*terms_a, *terms_c, fin, fmix]
    args += [follow] if q < parts - 1 else []
    args += [rim] if q == 0 else []
    shapes = [pltpu.VMEM((rows, cols), BF16)]
    shapes += [pltpu.VMEM((RIM, width), F32)] if q > 0 else []
    shapes += [pltpu.VMEM((RIM, width), BF16)] if q == parts - 1 else []
    return pl.pallas_call(
        functools.partial(finish_kernel, q, parts, n, len(terms_a), len(terms_c)),
        in_specs=[VMEM] * len(args),
        out_specs=[VMEM] * len(shapes),
        out_shape=shapes,
        scratch_shapes=[pltpu.VMEM((n + 2 * RIM, width), F32), pltpu.VMEM((80, LANES), F32)],
        compiler_params=params(),
        name="finish",
    )(*args)


def per_device(tokens, w_in, filt_in, filt_mix):
    rows = tokens.shape[0]
    cols = lax.axis_size("col")
    count = lax.axis_size("row")
    shape = side(count)
    n = rows // PARTS
    w = fetch(w_in)
    fin = filt_in.transpose(1, 0, 2)
    swap = [(c, c ^ 1) for c in range(cols)]
    outs, follow, rim = [], None, None
    for q in reversed(range(PARTS)):
        blocks = gather_tokens(tokens[q * n : (q + 1) * n], shape)
        mine = stack(blocks, shape)
        other = lax.ppermute(mine, "col", swap)
        sums = project(mine, other, w, n // 2, shape)
        terms_a, terms_c = exchange(sums, n // 2, shape)
        got = list(finish(q, PARTS, n, terms_a, terms_c, fin, filt_mix, follow, rim))
        outs.insert(0, got.pop(0))
        if q > 0:
            follow = got.pop(0)
        if q == PARTS - 1:
            rim = lax.ppermute(got.pop(0), "row", [(i, i + 1) for i in range(count - 1)])
    return jnp.concatenate(outs, axis=0)


def solution(mesh):
    return jax.shard_map(
        per_device,
        mesh=mesh,
        in_specs=(P("row", "col"), P("row", None, "col"), P(None, None, "col"), P(None, "col")),
        out_specs=P("row", "col"),
        check_vma=False,
    )
```

```python
import functools

import jax
import jax.numpy as jnp
from jax import lax
from jax.experimental import pallas as pl
from jax.experimental.pallas import tpu as pltpu
from jax.sharding import PartitionSpec as P

CORES = 2
RIM = 16
PARTS = 4
LANES = 128
VMEM = pl.BlockSpec(memory_space=pltpu.VMEM)
HBM = pl.BlockSpec(memory_space=pl.ANY)
BF16, F32 = jnp.bfloat16, jnp.float32


def params(mib=16):
    return pltpu.CompilerParams(vmem_limit_bytes=mib * 2**20)


QUICK = pl.CostEstimate(flops=1, bytes_accessed=1, transcendentals=0)


class Order:
    def __init__(self):
        self.last = None

    def call(self, kernel, args, shapes, name, scratch=(), specs=None):
        specs = [VMEM] * len(args) if specs is None else specs
        extra = [] if self.last is None else [self.last]
        count = len(args)

        def body(*refs):
            kernel(*refs[:count], *refs[count + len(extra) :])

        outs = pl.pallas_call(
            body,
            in_specs=specs + [HBM] * len(extra),
            out_specs=[VMEM] * len(shapes),
            out_shape=[pltpu.VMEM(s, t) for s, t in shapes],
            scratch_shapes=list(scratch),
            compiler_params=params(),
            cost_estimate=QUICK,
            name=name,
        )(*args, *extra)
        self.last = outs[-1]
        return list(outs)


def side(n):
    x = 1
    while x * x < n:
        x *= 2
    return n // x, x


def shift_rows(block, shape, dy, dx):
    ys, xs = shape
    route = []
    for y in range(ys):
        for x in range(xs):
            route.append((((y + dy) % ys) * xs + (x + dx) % xs, y * xs + x))
    return lax.ppermute(block, "row", route)


def shift_planes(block, dz):
    cols = lax.axis_size("col")
    return lax.ppermute(block, "col", [((c + CORES * dz) % cols, c) for c in range(cols)])


def fetch_kernel(w_ref, o_ref, sem):
    half = o_ref.shape[2]
    core = lax.rem(lax.axis_index("col"), CORES)
    copies = []
    for g in range(3):
        for j in range(2):
            start = pl.multiple_of((core if j == 0 else 1 - core) * half, half)
            copies.append(pltpu.make_async_copy(w_ref.at[g, pl.ds(start, half)], o_ref.at[g, j], sem.at[2 * g + j]))
    for c in copies:
        c.start()
    for c in copies:
        c.wait()


def fetch(order, w_in):
    w = pltpu.with_memory_space_constraint(w_in.transpose(1, 0, 2), pltpu.HBM)
    g, k, n = w.shape
    scratch = [pltpu.SemaphoreType.DMA((2 * g,))]
    return order.call(fetch_kernel, [w], [((g, 2, k // 2, n), BF16)], "fetch_w", scratch, specs=[HBM])[0]


def pick_kernel(shape, *refs):
    ys, xs = shape
    zs = ys * xs
    ins, outs = refs[:zs], refs[zs:]
    me = lax.axis_index("row")
    y, x = me // xs, lax.rem(me, xs)
    z = lax.axis_index("col") // CORES
    for dy in range(ys):
        for dx in range(xs):
            target = lax.rem(y - dy + ys, ys) * xs + lax.rem(x - dx + xs, xs)
            want = lax.rem(target - z + zs, zs)
            for dz in range(zs):

                @pl.when(want == dz)
                def _():
                    outs[dy * xs + dx][...] = ins[dz][...]


def gather_planes(piece, shape):
    ys, xs = shape
    return [piece] + [shift_planes(piece, dz) for dz in range(1, ys * xs)]


def gather_rows(order, strips, shape):
    xs = shape[1]
    picked = order.call(functools.partial(pick_kernel, shape), strips, [(strips[0].shape, BF16)] * len(strips), "pick")
    return [picked[0]] + [shift_rows(picked[i], shape, i // xs, i % xs) for i in range(1, len(picked))]


def stack_kernel(order, *refs):
    ins, out = refs[:-1], refs[-1]
    h = ins[0].shape[0] // 2
    for at, (block, part) in enumerate(order):
        out[at * h : (at + 1) * h] = ins[block][part * h : (part + 1) * h]


def stack(order, blocks, shape):
    ys, xs = shape
    parts = [(dy * xs + dx, 0) for dx in range(1, xs) for dy in range(ys)]
    parts += [(dy * xs + dx, 1) for dy in range(1, ys) for dx in range(xs)]
    parts += [(dy * xs, 0) for dy in range(ys)] + [(dx, 1) for dx in range(xs)]
    n, e = blocks[0].shape
    return order.call(functools.partial(stack_kernel, parts), blocks, [((len(blocks) * n, e), BF16)], "stack")[0]


def project_kernel(tn, mine, other, w_ref, *outs):
    n = w_ref.shape[3]
    for g in range(3):
        for j in range(n // tn):
            cols = slice(j * tn, (j + 1) * tn)
            acc = jnp.dot(mine[...], w_ref[g, 0, :, cols], preferred_element_type=F32)
            acc = acc + jnp.dot(other[...], w_ref[g, 1, :, cols], preferred_element_type=F32)
            at = 0
            for o in outs:
                o[:, g * n + j * tn : g * n + (j + 1) * tn] = acc[at : at + o.shape[0]].astype(o.dtype)
                at += o.shape[0]


def project(order, mine, other, w, h, shape):
    ys, xs = shape
    m, e = mine.shape
    cols = w.shape[3]
    shapes = [((ys * h, 3 * cols), BF16)] * (xs - 1) + [((xs * h, 3 * cols), BF16)] * (ys - 1)
    shapes += [((ys * h, 3 * cols), F32), ((xs * h, 3 * cols), F32)]
    outs = order.call(
        functools.partial(project_kernel, min(cols, 256)),
        [mine, other, w],
        shapes,
        "project",
    )
    got_a = [shift_rows(s, shape, 0, -dx) for dx, s in enumerate(outs[: xs - 1], 1)]
    got_c = [shift_rows(s, shape, -dy, 0) for dy, s in enumerate(outs[xs - 1 : -2], 1)]
    return [outs[-2], *got_a], [outs[-1], *got_c]


def middle_kernel(count_a, count_c, *refs):
    keep_a, got_a = refs[0], refs[1 : 1 + count_a]
    keep_c, got_c = refs[1 + count_a], refs[2 + count_a : 2 + count_a + count_c]
    outs = refs[2 + count_a + count_c :]
    h = outs[0].shape[0]
    for keep, got, mids in ((keep_a, got_a, outs[:count_c]), (keep_c, got_c, outs[count_c:])):
        for i, mid in enumerate(mids, 1):
            total = keep[i * h : (i + 1) * h]
            for g in got:
                total = total + g[i * h : (i + 1) * h].astype(F32)
            mid[...] = total.astype(BF16)


def middle(order, terms, h, shape):
    ys, xs = shape
    first, second = terms
    n = first[0].shape[1]
    mids = order.call(
        functools.partial(middle_kernel, xs - 1, ys - 1), [*first, *second], [((h, n), BF16)] * (xs + ys - 2), "middle"
    )
    last_a = [shift_rows(s, shape, -dy, 0) for dy, s in enumerate(mids[: ys - 1], 1)]
    last_c = [shift_rows(s, shape, 0, -dx) for dx, s in enumerate(mids[ys - 1 :], 1)]
    return [*first, *last_a], [*second, *last_c]


def finish_kernel(q, parts, n, count_a, count_c, *refs):
    refs = list(refs)
    terms = [refs[:count_a], refs[count_a : count_a + count_c]]
    del refs[: count_a + count_c]
    fin, fmix = refs.pop(0), refs.pop(0)
    follow = refs.pop(0) if q < parts - 1 else None
    rim = refs.pop(0) if q == 0 else None
    out = refs.pop(0)
    lead = refs.pop(0) if q > 0 else None
    tail = refs.pop(0) if q == parts - 1 else None
    ext, prod = refs
    h = n // 2
    for i, group in enumerate(terms):
        total = group[0][:h]
        for g in group[1:]:
            total = total + g[:h].astype(F32)
        ext[RIM + i * h : RIM + (i + 1) * h] = total
    if follow is not None:
        ext[RIM + n : RIM + n + RIM] = follow[...]
    if rim is not None:
        ext[:RIM] = rim[...].astype(F32)
    if lead is not None:
        lead[...] = ext[RIM : 2 * RIM]
    if tail is not None:
        tail[...] = ext[n : n + RIM].astype(BF16)
    cols = fmix.shape[1]
    first = RIM if q == 0 else 2 * RIM
    rows = out.shape[0]
    step = 48 if rows % 48 == 0 else (40 if rows % 40 == 0 else 16)
    step = min(step, rows)
    if rows % 64 == 0:
        step = 64

    def column(c, _):
        at = pl.multiple_of(c * LANES, LANES)

        def conv(g, start, count):
            where = pl.ds(pl.multiple_of(g * cols + at, LANES), LANES)
            total = fin[g, 0:1, pl.ds(at, LANES)] * ext[start : start + count, where]
            for s in range(1, 7):
                total = total + fin[g, s : s + 1, pl.ds(at, LANES)] * ext[start - s : start - s + count, where]
            return total

        for r in range(0, rows, step):
            base = first + r
            prod[: step + 8] = conv(1, base - 8, step + 8) * conv(2, base - 8, step + 8)
            mix = fmix[0:1, pl.ds(at, LANES)] * prod[8 : 8 + step]
            for s in range(1, 7):
                mix = mix + fmix[s : s + 1, pl.ds(at, LANES)] * prod[8 - s : 8 - s + step]
            out[r : r + step, pl.ds(at, LANES)] = (conv(0, base, step) * mix).astype(BF16)
        return 0

    lax.fori_loop(0, cols // LANES, column, 0)


def finish(order, q, parts, n, terms, fin, fmix, follow, rim):
    width = terms[0][0].shape[1]
    cols = fmix.shape[1]
    rows = n + (RIM if q == 0 else 0) - (RIM if q == parts - 1 else 0)
    args = [*terms[0], *terms[1], fin, fmix]
    args += [follow] if q < parts - 1 else []
    args += [rim] if q == 0 else []
    shapes = [((rows, cols), BF16)]
    shapes += [((RIM, width), F32)] if q > 0 else []
    shapes += [((RIM, width), BF16)] if q == parts - 1 else []
    kernel = functools.partial(finish_kernel, q, parts, n, len(terms[0]), len(terms[1]))
    scratch = [pltpu.VMEM((n + 2 * RIM, width), F32), pltpu.VMEM((80, LANES), F32)]
    return order.call(kernel, args, shapes, "finish", scratch)


PLAN = "P0 W K0 P1 J0 K1 P2 J1 M0 K2 P3 J2 M1 K3 F0 J3 M2 F1 M3 F2 F3"


def per_device(tokens, w_in, filt_in, filt_mix):
    rows = tokens.shape[0]
    cols = lax.axis_size("col")
    count = lax.axis_size("row")
    shape = side(count)
    n = rows // PARTS
    order = Order()
    fin = filt_in.transpose(1, 0, 2)
    swap = [(c, c ^ 1) for c in range(cols)]
    pieces = [tokens[(PARTS - 1 - i) * n : (PARTS - i) * n] for i in range(PARTS)]
    strips = [gather_planes(piece, shape) for piece in pieces]
    blocks, mine, other, terms, outs = {}, {}, {}, {}, {}
    follow, rim = None, None
    for step in PLAN.split():
        kind, i = step[0], int(step[1:] or 0)
        if kind == "W":
            w = fetch(order, w_in)
        elif kind == "P":
            blocks[i] = gather_rows(order, strips[i], shape)
        elif kind == "K":
            mine[i] = stack(order, blocks[i], shape)
            other[i] = lax.ppermute(mine[i], "col", swap)
        elif kind == "J":
            terms[i] = project(order, mine[i], other[i], w, n // 2, shape)
        elif kind == "M":
            terms[i] = middle(order, terms[i], n // 2, shape)
        else:
            q = PARTS - 1 - i
            got = finish(order, q, PARTS, n, terms[i], fin, filt_mix, follow, rim)
            outs[q] = got.pop(0)
            if q > 0:
                follow = got.pop(0)
            if i == 0:
                rim = lax.ppermute(got.pop(0), "row", [(r, r + 1) for r in range(count - 1)])
    return jnp.concatenate([outs[q] for q in range(PARTS)], axis=0)


def solution(mesh):
    return jax.shard_map(
        per_device,
        mesh=mesh,
        in_specs=(P("row", "col"), P("row", None, "col"), P(None, None, "col"), P(None, "col")),
        out_specs=P("row", "col"),
        check_vma=False,
    )
```

```python
import functools

import jax
import jax.numpy as jnp
from jax import lax
from jax.experimental import pallas as pl
from jax.experimental.pallas import tpu as pltpu
from jax.sharding import PartitionSpec as P

CORES = 2
RIM = 16
STEP = 72
LANES = 128
VMEM = pl.BlockSpec(memory_space=pltpu.VMEM)
HBM = pl.BlockSpec(memory_space=pl.ANY)
BF16, F32 = jnp.bfloat16, jnp.float32


def params(mib=16):
    return pltpu.CompilerParams(vmem_limit_bytes=mib * 2**20)


class Order:
    def __init__(self):
        self.last = None
        self.wait = []

    def call(self, kernel, args, shapes, name, scratch=(), specs=None, after=(), shown=0):
        specs = [VMEM] * len(args) if specs is None else specs
        extra = [*([] if self.last is None else [self.last]), *self.wait, *after]
        self.wait = []
        count = len(args)

        def body(*refs):
            kernel(*refs[:count], *refs[count + len(extra) :])

        outs = pl.pallas_call(
            body,
            in_specs=specs + [HBM] * len(extra),
            out_specs=[VMEM] * len(shapes),
            out_shape=[pltpu.VMEM(s, t) for s, t in shapes],
            scratch_shapes=list(scratch),
            compiler_params=params(),
            cost_estimate=pl.CostEstimate(flops=shown, bytes_accessed=0, transcendentals=0),
            name=name,
        )(*args, *extra)
        self.last = outs[-1]
        return list(outs)


def side(n):
    x = 1
    while x * x < n:
        x *= 2
    return n // x, x


def shift_rows(block, shape, dy, dx):
    ys, xs = shape
    route = []
    for y in range(ys):
        for x in range(xs):
            route.append((((y + dy) % ys) * xs + (x + dx) % xs, y * xs + x))
    return lax.ppermute(block, "row", route)


def widen_kernel(own, other, *outs):
    e = own.shape[1]
    core = lax.rem(lax.axis_index("col"), CORES)
    row = own.shape[0]
    for o in outs:
        row -= o.shape[0]
        for k in range(CORES):

            @pl.when(core == k)
            def _():
                o[:, k * e : (k + 1) * e] = own[row : row + o.shape[0]]
                o[:, (1 - k) * e : (2 - k) * e] = other[row : row + o.shape[0]]


def widen(order, own, other, sizes):
    shapes = [((n, CORES * own.shape[1]), BF16) for n in sizes]
    return order.call(widen_kernel, [own, other], shapes, "widen")


def gather(piece):
    count, cols = lax.axis_size("row"), lax.axis_size("col")
    planes = cols // CORES
    assert count == planes and count & (count - 1) == 0

    def place(row, plane, core):
        return row * cols + plane * CORES + core

    blocks = []
    for a in range(count // CORES):
        route = []
        for row in range(count):
            for plane in range(planes):
                for core in range(CORES):
                    route.append((place(row, plane, core), place(plane, row ^ (a * CORES + core), core)))
        blocks.append(lax.ppermute(piece, ("row", "col"), route))
    return blocks


def cut_kernel(sizes, count, *refs):
    outs = iter(refs[count:])
    for block in refs[:count]:
        end = block.shape[0]
        for n in sizes:
            next(outs)[...] = block[end - n : end]
            end -= n


def cut(order, blocks, sizes):
    e = blocks[0].shape[1]
    kernel = functools.partial(cut_kernel, sizes, len(blocks))
    outs = order.call(kernel, blocks, [((n, e), BF16) for _ in blocks for n in sizes], "cut")
    return [outs[i :: len(sizes)] for i in range(len(sizes))]


def stack_halves(shape, mine, other, out):
    ys, xs = shape
    h = out.shape[1]
    me = lax.axis_index("row")
    plane = lax.axis_index("col") // CORES
    core = lax.rem(lax.axis_index("col"), CORES)
    sent = (xs - 1) * ys + (ys - 1) * xs
    for a in range(len(mine)):
        for blocks, j in ((mine, a * CORES + core), (other, a * CORES + 1 - core)):
            row = lax.bitwise_xor(plane, j)
            dy = lax.rem(row // xs - me // xs + ys, ys)
            dx = lax.rem(lax.rem(row, xs) - lax.rem(me, xs) + xs, xs)
            out[jnp.where(dx > 0, (dx - 1) * ys + dy, sent + dy)] = blocks[a][:h]
            out[jnp.where(dy > 0, (xs - 1) * ys + (dy - 1) * xs + dx, sent + ys + dx)] = blocks[a][h:]


def fetch_kernel(w_ref, o_ref, sems):
    copies = [pltpu.make_async_copy(w_ref.at[g], o_ref.at[g], sems.at[g]) for g in range(3)]
    for c in copies:
        c.start()
    for c in copies:
        c.wait()


def fetch(order, w_in):
    w = pltpu.with_memory_space_constraint(w_in.transpose(1, 0, 2), pltpu.HBM)
    scratch = [pltpu.SemaphoreType.DMA((3,))]
    return order.call(fetch_kernel, [w], [(w.shape, BF16)], "fetch_w", scratch, specs=[HBM])[0]


def project_kernel(tn, shape, *refs):
    count = shape[0] * shape[1] // CORES
    mine, other, w_ref = refs[:count], refs[count : 2 * count], refs[2 * count]
    *outs, halves = refs[2 * count + 1 :]
    stack_halves(shape, mine, other, halves)
    parts, h, e = halves.shape
    cols = w_ref.shape[2]
    for g in range(3):
        for c in range(0, cols, tn):
            acc = jnp.dot(halves[...].reshape(parts * h, e), w_ref[g, :, c : c + tn], preferred_element_type=F32)
            at = 0
            for o in outs:
                o[:, g * cols + c : g * cols + c + tn] = acc[at : at + o.shape[0]].astype(o.dtype)
                at += o.shape[0]


def project(order, mine, other, w, shape):
    ys, xs = shape
    n, e = mine[0].shape
    h = n // 2
    cols = w.shape[2]
    counts = [ys] * (xs - 1) + [xs] * (ys - 1) + [ys, xs]
    shapes = [((k * h, 3 * cols), BF16 if i < xs + ys - 2 else F32) for i, k in enumerate(counts)]
    scratch = [pltpu.VMEM((2 * xs * ys, h, e), BF16)]
    kernel = functools.partial(project_kernel, min(cols, 256), shape)
    outs = order.call(kernel, [*mine, *other, w], shapes, "project", scratch)
    got_a = [shift_rows(s, shape, 0, -dx) for dx, s in enumerate(outs[: xs - 1], 1)]
    got_c = [shift_rows(s, shape, -dy, 0) for dy, s in enumerate(outs[xs - 1 : -2], 1)]
    return [outs[-2], *got_a], [outs[-1], *got_c]


def middle_kernel(count_a, count_c, *refs):
    keep_a, got_a = refs[0], refs[1 : 1 + count_a]
    keep_c, got_c = refs[1 + count_a], refs[2 + count_a : 2 + count_a + count_c]
    outs = refs[2 + count_a + count_c :]
    h = outs[0].shape[0]
    for keep, got, mids in ((keep_a, got_a, outs[:count_c]), (keep_c, got_c, outs[count_c:])):
        for i, mid in enumerate(mids, 1):
            total = keep[i * h : (i + 1) * h]
            for g in got:
                total = total + g[i * h : (i + 1) * h].astype(F32)
            mid[...] = total.astype(BF16)


def middle(order, terms, h, shape):
    ys, xs = shape
    first, second = terms
    n = first[0].shape[1]
    mids = order.call(
        functools.partial(middle_kernel, xs - 1, ys - 1), [*first, *second], [((h, n), BF16)] * (xs + ys - 2), "middle"
    )
    last_a = [shift_rows(s, shape, -dy, 0) for dy, s in enumerate(mids[: ys - 1], 1)]
    last_c = [shift_rows(s, shape, 0, -dx) for dx, s in enumerate(mids[ys - 1 :], 1)]
    return [*first, *last_a], [*second, *last_c]


def finish_kernel(top, bottom, n, count_a, count_c, *refs):
    refs = list(refs)
    terms = [refs[:count_a], refs[count_a : count_a + count_c]]
    del refs[: count_a + count_c]
    fin, fmix = refs.pop(0), refs.pop(0)
    follow = refs.pop(0) if not bottom else None
    rim = refs.pop(0) if top else None
    out = refs.pop(0)
    lead = refs.pop(0) if not top else None
    tail = refs.pop(0) if bottom else None
    ext, prod = refs
    h = n // 2
    for i, group in enumerate(terms):
        total = group[0][:h]
        for g in group[1:]:
            total = total + g[:h].astype(F32)
        ext[RIM + i * h : RIM + (i + 1) * h] = total
    if follow is not None:
        ext[RIM + n : RIM + n + RIM] = follow[...]
    if rim is not None:
        ext[:RIM] = rim[...].astype(F32)
    if lead is not None:
        lead[...] = ext[RIM : 2 * RIM]
    if tail is not None:
        tail[...] = ext[n : n + RIM].astype(BF16)
    cols = fmix.shape[1]
    first = RIM if top else 2 * RIM
    rows = out.shape[0]
    step = max(s for s in range(16, STEP + 1, 8) if rows % s == 0)

    def column(c, _):
        at = pl.multiple_of(c * LANES, LANES)

        def conv(g, start, count):
            where = pl.ds(pl.multiple_of(g * cols + at, LANES), LANES)
            total = fin[g, 0:1, pl.ds(at, LANES)] * ext[start : start + count, where]
            for s in range(1, 7):
                total = total + fin[g, s : s + 1, pl.ds(at, LANES)] * ext[start - s : start - s + count, where]
            return total

        for r in range(0, rows, step):
            base = first + r
            prod[: step + 8] = conv(1, base - 8, step + 8) * conv(2, base - 8, step + 8)
            mix = fmix[0:1, pl.ds(at, LANES)] * prod[8 : 8 + step]
            for s in range(1, 7):
                mix = mix + fmix[s : s + 1, pl.ds(at, LANES)] * prod[8 - s : 8 - s + step]
            out[r : r + step, pl.ds(at, LANES)] = (conv(0, base, step) * mix).astype(BF16)
        return 0

    lax.fori_loop(0, cols // LANES, column, 0)


def finish(order, top, bottom, n, terms, fin, fmix, follow, rim):
    width = terms[0][0].shape[1]
    cols = fmix.shape[1]
    rows = n + (RIM if top else 0) - (RIM if bottom else 0)
    args = [*terms[0], *terms[1], fin, fmix]
    args += [follow] if not bottom else []
    args += [rim] if top else []
    shapes = [((rows, cols), BF16)]
    shapes += [((RIM, width), F32)] if not top else []
    shapes += [((RIM, width), BF16)] if bottom else []
    kernel = functools.partial(finish_kernel, top, bottom, n, len(terms[0]), len(terms[1]))
    scratch = [pltpu.VMEM((n + 2 * RIM, width), F32), pltpu.VMEM((STEP + 8, LANES), F32)]
    return order.call(kernel, args, shapes, "finish", scratch, shown=50 * 10**9 if bottom else 0)


CHUNKS = ((3,), (3, 2))
PLAN = ("W", "K0", "C0", "J0", "K1", "C1", "C2", "M0", "J1", "F0", "J2", "M1", "M2", "F1", "F2")


def per_device(tokens, w_in, filt_in, filt_mix):
    rows = tokens.shape[0]
    cols = lax.axis_size("col")
    count = lax.axis_size("row")
    shape = side(count)
    order = Order()
    fin = filt_in.transpose(1, 0, 2)
    swap = [(c, c ^ 1) for c in range(cols)]
    parts = [[rows * k // 8 for k in chunk] for chunk in CHUNKS]
    sizes = sum(parts, [])
    last = len(sizes) - 1
    wide = widen(order, tokens, lax.ppermute(tokens, "col", swap), [sum(p) for p in parts])
    blocks = [gather(piece) for piece in wide]
    mine, other, terms, outs = [], {}, {}, {}
    follow, rim = None, None
    for step in PLAN:
        kind, i = step[0], int(step[1:] or 0)
        if kind == "W":
            w = fetch(order, w_in)
        elif kind == "K":
            mine += cut(order, blocks[i], parts[i])
        elif kind == "C":
            other[i] = [lax.ppermute(b, "col", swap) for b in mine[i]]
        elif kind == "J":
            terms[i] = project(order, mine[i], other[i], w, shape)
        elif kind == "M":
            terms[i] = middle(order, terms[i], sizes[i] // 2, shape)
        else:
            got = finish(order, i == last, i == 0, sizes[i], terms[i], fin, filt_mix, follow, rim)
            outs[i] = got.pop(0)
            if i < last:
                follow = got.pop(0)
            if i == 0:
                rim = lax.ppermute(got.pop(0), "row", [(r, r + 1) for r in range(count - 1)])
    return jnp.concatenate([outs[i] for i in reversed(range(len(sizes)))], axis=0)


def solution(mesh):
    return jax.shard_map(
        per_device,
        mesh=mesh,
        in_specs=(P("row", "col"), P("row", None, "col"), P(None, None, "col"), P(None, "col")),
        out_specs=P("row", "col"),
        check_vma=False,
    )
```

```python
import functools

import jax
import jax.numpy as jnp
from jax import lax
from jax.experimental import pallas as pl
from jax.experimental.pallas import tpu as pltpu
from jax.sharding import PartitionSpec as P

CORES = 2
RIM = 16
STEP = 72
LANES = 128
LONG = 10 * 10**9
VMEM = pl.BlockSpec(memory_space=pltpu.VMEM)
HBM = pl.BlockSpec(memory_space=pl.ANY)
BF16, F32 = jnp.bfloat16, jnp.float32


def params(mib=16):
    return pltpu.CompilerParams(vmem_limit_bytes=mib * 2**20)


class Order:
    def __init__(self):
        self.last = None
        self.wait = []

    def call(self, kernel, args, shapes, name, scratch=(), specs=None, shown=0, last=False):
        specs = [VMEM] * len(args) if specs is None else specs
        extra = [*([] if self.last is None else [self.last]), *self.wait]
        self.wait = []
        count = len(args)

        def body(*refs):
            kernel(*refs[:count], *refs[count + len(extra) :])

        outs = pl.pallas_call(
            body,
            in_specs=specs + [HBM] * len(extra),
            out_specs=[HBM if last else VMEM] * len(shapes),
            out_shape=[jax.ShapeDtypeStruct(s, t) if last else pltpu.VMEM(s, t) for s, t in shapes],
            scratch_shapes=list(scratch),
            compiler_params=params(),
            cost_estimate=pl.CostEstimate(flops=shown, bytes_accessed=0, transcendentals=0),
            name=name,
        )(*args, *extra)
        self.last = outs[-1]
        return list(outs)


def side(n):
    x = 1
    while x * x < n:
        x *= 2
    return n // x, x


def shift_rows(block, shape, dy, dx):
    ys, xs = shape
    route = []
    for y in range(ys):
        for x in range(xs):
            route.append((((y + dy) % ys) * xs + (x + dx) % xs, y * xs + x))
    return lax.ppermute(block, "row", route)


def widen_kernel(own, other, *refs):
    *outs, sems = refs
    e = own.shape[1]
    core = lax.rem(lax.axis_index("col"), CORES)
    for k in range(CORES):

        @pl.when(core == k)
        def _():
            copies = []
            row = own.shape[0]
            for i, o in enumerate(outs):
                row -= o.shape[0]
                source = own.at[pl.ds(row, o.shape[0])]
                copies.append(pltpu.make_async_copy(source, o.at[:, pl.ds(k * e, e)], sems.at[i]))
            for c in copies:
                c.start()
            row = own.shape[0]
            for o in outs:
                row -= o.shape[0]
                o[:, (1 - k) * e : (2 - k) * e] = other[row : row + o.shape[0]]
            for c in copies:
                c.wait()


def widen(order, own, other, sizes):
    shapes = [((n, CORES * own.shape[1]), BF16) for n in sizes]
    own = pltpu.with_memory_space_constraint(own, pltpu.HBM)
    scratch = [pltpu.SemaphoreType.DMA((len(sizes),))]
    return order.call(widen_kernel, [own, other], shapes, "widen", scratch, specs=[HBM, VMEM])


def gather(piece):
    count, cols = lax.axis_size("row"), lax.axis_size("col")
    planes = cols // CORES
    assert count == planes and count & (count - 1) == 0

    def place(row, plane, core):
        return row * cols + plane * CORES + core

    blocks = []
    for a in range(count // CORES):
        route = []
        for row in range(count):
            for plane in range(planes):
                for core in range(CORES):
                    route.append((place(row, plane, core), place(plane, row ^ (a * CORES + core), core)))
        blocks.append(lax.ppermute(piece, ("row", "col"), route))
    return blocks


def cut_kernel(sizes, count, *refs):
    outs = iter(refs[count:])
    for block in refs[:count]:
        end = block.shape[0]
        for n in sizes:
            next(outs)[...] = block[end - n : end]
            end -= n


def cut(order, blocks, sizes):
    e = blocks[0].shape[1]
    kernel = functools.partial(cut_kernel, sizes, len(blocks))
    outs = order.call(kernel, blocks, [((n, e), BF16) for _ in blocks for n in sizes], "cut")
    return [outs[i :: len(sizes)] for i in range(len(sizes))]


def stack_halves(shape, mine, other, out):
    ys, xs = shape
    h = out.shape[1]
    me = lax.axis_index("row")
    plane = lax.axis_index("col") // CORES
    core = lax.rem(lax.axis_index("col"), CORES)
    sent = (xs - 1) * ys + (ys - 1) * xs
    for a in range(len(mine)):
        for blocks, j in ((mine, a * CORES + core), (other, a * CORES + 1 - core)):
            row = lax.bitwise_xor(plane, j)
            dy = lax.rem(row // xs - me // xs + ys, ys)
            dx = lax.rem(lax.rem(row, xs) - lax.rem(me, xs) + xs, xs)
            out[jnp.where(dx > 0, (dx - 1) * ys + dy, sent + dy)] = blocks[a][:h]
            out[jnp.where(dy > 0, (xs - 1) * ys + (dy - 1) * xs + dx, sent + ys + dx)] = blocks[a][h:]


def fetch_kernel(w_ref, o_ref, sems):
    copies = [pltpu.make_async_copy(w_ref.at[g], o_ref.at[g], sems.at[g]) for g in range(3)]
    for c in copies:
        c.start()
    for c in copies:
        c.wait()


def fetch(order, w_in):
    w = pltpu.with_memory_space_constraint(w_in.transpose(1, 0, 2), pltpu.HBM)
    scratch = [pltpu.SemaphoreType.DMA((3,))]
    return order.call(fetch_kernel, [w], [(w.shape, BF16)], "fetch_w", scratch, specs=[HBM])[0]


def project_kernel(tn, shape, start, *refs):
    count = shape[0] * shape[1] // CORES
    mine, other, w_ref = refs[:count], refs[count : 2 * count], refs[2 * count]
    *outs, halves = refs[2 * count + 1 :]
    stack_halves(shape, mine, other, halves)
    h, e = halves.shape[1:]
    rows = sum(o.shape[0] for o in outs)
    cols = w_ref.shape[2]
    for g in range(3):
        for c in range(0, cols, tn):
            x = halves[start : start + rows // h].reshape(rows, e)
            acc = jnp.dot(x, w_ref[g, :, c : c + tn], preferred_element_type=F32)
            at = 0
            for o in outs:
                o[:, g * cols + c : g * cols + c + tn] = acc[at : at + o.shape[0]].astype(o.dtype)
                at += o.shape[0]


def project(order, mine, other, w, shape, kept):
    ys, xs = shape
    n, e = mine[0].shape
    h = n // 2
    cols = w.shape[2]
    sent = [ys] * (xs - 1) + [xs] * (ys - 1)
    shapes = [((k * h, 3 * cols), F32 if kept else BF16) for k in ([ys, xs] if kept else sent)]
    scratch = [pltpu.VMEM((2 * xs * ys, h, e), BF16)]
    kernel = functools.partial(project_kernel, min(cols, 256), shape, sum(sent) if kept else 0)
    outs = order.call(kernel, [*mine, *other, w], shapes, "keep" if kept else "send", scratch, shown=LONG if kept else 0)
    if kept:
        return outs
    got_a = [shift_rows(s, shape, 0, -dx) for dx, s in enumerate(outs[: xs - 1], 1)]
    got_c = [shift_rows(s, shape, -dy, 0) for dy, s in enumerate(outs[xs - 1 :], 1)]
    return got_a, got_c


def middle_kernel(count_a, count_c, *refs):
    keep_a, got_a = refs[0], refs[1 : 1 + count_a]
    keep_c, got_c = refs[1 + count_a], refs[2 + count_a : 2 + count_a + count_c]
    outs = refs[2 + count_a + count_c :]
    h = outs[0].shape[0]
    for keep, got, mids in ((keep_a, got_a, outs[:count_c]), (keep_c, got_c, outs[count_c:])):
        for i, mid in enumerate(mids, 1):
            total = keep[i * h : (i + 1) * h]
            for g in got:
                total = total + g[i * h : (i + 1) * h].astype(F32)
            mid[...] = total.astype(BF16)


def middle(order, terms, h, shape):
    ys, xs = shape
    first, second = terms
    n = first[0].shape[1]
    mids = order.call(
        functools.partial(middle_kernel, xs - 1, ys - 1), [*first, *second], [((h, n), BF16)] * (xs + ys - 2), "middle"
    )
    last_a = [shift_rows(s, shape, -dy, 0) for dy, s in enumerate(mids[: ys - 1], 1)]
    last_c = [shift_rows(s, shape, 0, -dx) for dx, s in enumerate(mids[ys - 1 :], 1)]
    return [*first, *last_a], [*second, *last_c]


def finish_kernel(top, bottom, n, count_a, count_c, dones, *refs):
    refs = list(refs)
    terms = [refs[:count_a], refs[count_a : count_a + count_c]]
    del refs[: count_a + count_c]
    fin, fmix = refs.pop(0), refs.pop(0)
    follow = refs.pop(0) if not bottom else None
    rim = refs.pop(0) if top else None
    done = [refs.pop(0) for _ in range(dones)]
    out = refs.pop(0)
    lead = refs.pop(0) if not top else None
    tail = refs.pop(0) if bottom else None
    copies = []
    if top:
        whole, out, sems = out, refs.pop(), refs.pop()
        row = whole.shape[0]
        for i, o in enumerate([*done, out]):
            row -= o.shape[0]
            copies.append(pltpu.make_async_copy(o, whole.at[pl.ds(row, o.shape[0])], sems.at[i]))
        for c in copies[:-1]:
            c.start()
    ext, prod = refs
    h = n // 2
    for i, group in enumerate(terms):
        total = group[0][:h]
        for g in group[1:]:
            total = total + g[:h].astype(F32)
        ext[RIM + i * h : RIM + (i + 1) * h] = total
    if follow is not None:
        ext[RIM + n : RIM + n + RIM] = follow[...]
    if rim is not None:
        ext[:RIM] = rim[...].astype(F32)
    if lead is not None:
        lead[...] = ext[RIM : 2 * RIM]
    if tail is not None:
        tail[...] = ext[n : n + RIM].astype(BF16)
    cols = fmix.shape[1]
    first = RIM if top else 2 * RIM
    rows = out.shape[0]
    step = max(s for s in range(16, STEP + 1, 8) if rows % s == 0)

    def column(c, _):
        at = pl.multiple_of(c * LANES, LANES)

        def conv(g, start, count):
            where = pl.ds(pl.multiple_of(g * cols + at, LANES), LANES)
            total = fin[g, 0:1, pl.ds(at, LANES)] * ext[start : start + count, where]
            for s in range(1, 7):
                total = total + fin[g, s : s + 1, pl.ds(at, LANES)] * ext[start - s : start - s + count, where]
            return total

        for r in range(0, rows, step):
            base = first + r
            prod[: step + 8] = conv(1, base - 8, step + 8) * conv(2, base - 8, step + 8)
            mix = fmix[0:1, pl.ds(at, LANES)] * prod[8 : 8 + step]
            for s in range(1, 7):
                mix = mix + fmix[s : s + 1, pl.ds(at, LANES)] * prod[8 - s : 8 - s + step]
            out[r : r + step, pl.ds(at, LANES)] = (conv(0, base, step) * mix).astype(BF16)
        return 0

    lax.fori_loop(0, cols // LANES, column, 0)
    for c in copies[-1:]:
        c.start()
    for c in copies:
        c.wait()


def finish(order, top, bottom, n, terms, fin, fmix, follow, rim, done):
    width = terms[0][0].shape[1]
    cols = fmix.shape[1]
    rows = n + (RIM if top else 0) - (RIM if bottom else 0)
    args = [*terms[0], *terms[1], fin, fmix]
    args += [follow] if not bottom else []
    args += [rim, *done] if top else []
    height = rows + sum(o.shape[0] for o in done)
    shapes = [((height if top else rows, cols), BF16)]
    shapes += [((RIM, width), F32)] if not top else []
    shapes += [((RIM, width), BF16)] if bottom else []
    kernel = functools.partial(finish_kernel, top, bottom, n, len(terms[0]), len(terms[1]), len(done) if top else 0)
    scratch = [pltpu.VMEM((n + 2 * RIM, width), F32), pltpu.VMEM((STEP + 8, LANES), F32)]
    scratch += [pltpu.SemaphoreType.DMA((len(done) + 1,)), pltpu.VMEM((rows, cols), BF16)] if top else []
    return order.call(kernel, args, shapes, "finish", scratch, shown=LONG if bottom else 0, last=top)


CHUNKS = ((3,), (3, 2))
PLAN = ("W", "K0", "C0", "J0", "B0", "K1", "C1", "C2", "M0", "Y2", "J1", "B1", "F0", "J2", "B2", "M1", "M2", "F1", "F2")


def per_device(tokens, w_in, filt_in, filt_mix):
    rows = tokens.shape[0]
    cols = lax.axis_size("col")
    count = lax.axis_size("row")
    shape = side(count)
    order = Order()
    fin = filt_in.transpose(1, 0, 2)
    swap = [(c, c ^ 1) for c in range(cols)]
    parts = [[rows * k // 8 for k in chunk] for chunk in CHUNKS]
    sizes = sum(parts, [])
    last = len(sizes) - 1
    wide = widen(order, tokens, lax.ppermute(tokens, "col", swap), [sum(p) for p in parts])
    blocks = [gather(piece) for piece in wide]
    mine, outs, other, got, terms = [], [], {}, {}, {}
    follow, rim = None, None
    for step in PLAN:
        kind, i = step[0], int(step[1:] or 0)
        if kind == "W":
            w = fetch(order, w_in)
        elif kind == "Y":
            order.wait += other[i]
        elif kind == "K":
            mine += cut(order, blocks[i], parts[i])
        elif kind == "C":
            other[i] = [lax.ppermute(b, "col", swap) for b in mine[i]]
        elif kind == "J":
            got[i] = project(order, mine[i], other[i], w, shape, False)
        elif kind == "B":
            keep = project(order, mine[i], other[i], w, shape, True)
            terms[i] = [[k, *g] for k, g in zip(keep, got[i])]
        elif kind == "M":
            terms[i] = middle(order, terms[i], sizes[i] // 2, shape)
        else:
            made = finish(order, i == last, i == 0, sizes[i], terms[i], fin, filt_mix, follow, rim, outs)
            outs.append(made.pop(0))
            if i < last:
                follow = made.pop(0)
            if i == 0:
                rim = lax.ppermute(made.pop(0), "row", [(r, r + 1) for r in range(count - 1)])
    return outs[-1]


def solution(mesh):
    return jax.shard_map(
        per_device,
        mesh=mesh,
        in_specs=(P("row", "col"), P("row", None, "col"), P(None, None, "col"), P(None, "col")),
        out_specs=P("row", "col"),
        check_vma=False,
    )
```

```python
import functools

import jax
import jax.numpy as jnp
from jax import lax
from jax.experimental import pallas as pl
from jax.experimental.pallas import tpu as pltpu
from jax.sharding import PartitionSpec as P

CORES = 2
RIM = 16
STEP = 72
LANES = 128
LONG = 10 * 10**9
VMEM = pl.BlockSpec(memory_space=pltpu.VMEM)
HBM = pl.BlockSpec(memory_space=pl.ANY)
BF16, F32 = jnp.bfloat16, jnp.float32


def params(mib=16):
    return pltpu.CompilerParams(vmem_limit_bytes=mib * 2**20)


class Order:
    def __init__(self):
        self.last = None
        self.wait = []

    def call(self, kernel, args, shapes, name, scratch=(), specs=None, shown=0, last=False):
        specs = [VMEM] * len(args) if specs is None else specs
        extra = [*([] if self.last is None else [self.last]), *self.wait]
        self.wait = []
        count = len(args)

        def body(*refs):
            kernel(*refs[:count], *refs[count + len(extra) :])

        outs = pl.pallas_call(
            body,
            in_specs=specs + [HBM] * len(extra),
            out_specs=[HBM if last else VMEM] * len(shapes),
            out_shape=[jax.ShapeDtypeStruct(s, t) if last else pltpu.VMEM(s, t) for s, t in shapes],
            scratch_shapes=list(scratch),
            compiler_params=params(),
            cost_estimate=pl.CostEstimate(flops=shown, bytes_accessed=0, transcendentals=0),
            name=name,
        )(*args, *extra)
        self.last = outs[-1]
        return list(outs)


def side(n):
    x = 1
    while x * x < n:
        x *= 2
    return n // x, x


def shift_rows(block, shape, dy, dx):
    ys, xs = shape
    route = []
    for y in range(ys):
        for x in range(xs):
            route.append((((y + dy) % ys) * xs + (x + dx) % xs, y * xs + x))
    return lax.ppermute(block, "row", route)


def widen_kernel(own, other, *refs):
    *outs, sems = refs
    e = own.shape[1]
    core = lax.rem(lax.axis_index("col"), CORES)
    for k in range(CORES):

        @pl.when(core == k)
        def _():
            copies = []
            row = own.shape[0]
            for i, o in enumerate(outs):
                row -= o.shape[0]
                source = own.at[pl.ds(row, o.shape[0])]
                copies.append(pltpu.make_async_copy(source, o.at[:, pl.ds(k * e, e)], sems.at[i]))
            for c in copies:
                c.start()
            row = own.shape[0]
            for o in outs:
                row -= o.shape[0]
                o[:, (1 - k) * e : (2 - k) * e] = other[row : row + o.shape[0]]
            for c in copies:
                c.wait()


def widen(order, own, other, sizes):
    shapes = [((n, CORES * own.shape[1]), BF16) for n in sizes]
    own = pltpu.with_memory_space_constraint(own, pltpu.HBM)
    scratch = [pltpu.SemaphoreType.DMA((len(sizes),))]
    return order.call(widen_kernel, [own, other], shapes, "widen", scratch, specs=[HBM, VMEM])


def gather(piece):
    count, cols = lax.axis_size("row"), lax.axis_size("col")
    planes = cols // CORES
    assert count == planes and count & (count - 1) == 0

    def place(row, plane, core):
        return row * cols + plane * CORES + core

    blocks = []
    for a in range(count // CORES):
        route = []
        for row in range(count):
            for plane in range(planes):
                for core in range(CORES):
                    route.append((place(row, plane, core), place(plane, row ^ (core * (count // CORES) + a), core)))
        blocks.append(lax.ppermute(piece, ("row", "col"), route))
    return blocks


def cut_kernel(sizes, count, *refs):
    outs = iter(refs[count:])
    for block in refs[:count]:
        end = block.shape[0]
        for n in sizes:
            next(outs)[...] = block[end - n : end]
            end -= n


def cut(order, blocks, sizes):
    e = blocks[0].shape[1]
    kernel = functools.partial(cut_kernel, sizes, len(blocks))
    outs = order.call(kernel, blocks, [((n, e), BF16) for _ in blocks for n in sizes], "cut")
    return [outs[i :: len(sizes)] for i in range(len(sizes))]


def stack_halves(shape, mine, other, out):
    ys, xs = shape
    h = out.shape[1]
    me = lax.axis_index("row")
    plane = lax.axis_index("col") // CORES
    core = lax.rem(lax.axis_index("col"), CORES)
    sent = (xs - 1) * ys + (ys - 1) * xs
    for a in range(len(mine)):
        for blocks, j in ((mine, core * len(mine) + a), (other, (1 - core) * len(mine) + a)):
            row = lax.bitwise_xor(plane, j)
            dy = lax.rem(row // xs - me // xs + ys, ys)
            dx = lax.rem(lax.rem(row, xs) - lax.rem(me, xs) + xs, xs)
            out[jnp.where(dx > 0, (dx - 1) * ys + dy, sent + dy)] = blocks[a][:h]
            out[jnp.where(dy > 0, (xs - 1) * ys + (dy - 1) * xs + dx, sent + ys + dx)] = blocks[a][h:]


def fetch_kernel(w_ref, o_ref, sems):
    copies = [pltpu.make_async_copy(w_ref.at[g], o_ref.at[g], sems.at[g]) for g in range(3)]
    for c in copies:
        c.start()
    for c in copies:
        c.wait()


def fetch(order, w_in):
    w = pltpu.with_memory_space_constraint(w_in.transpose(1, 0, 2), pltpu.HBM)
    scratch = [pltpu.SemaphoreType.DMA((3,))]
    return order.call(fetch_kernel, [w], [(w.shape, BF16)], "fetch_w", scratch, specs=[HBM])[0]


def project_kernel(tn, shape, start, *refs):
    count = shape[0] * shape[1] // CORES
    mine, other, w_ref = refs[:count], refs[count : 2 * count], refs[2 * count]
    *outs, halves = refs[2 * count + 1 :]
    stack_halves(shape, mine, other, halves)
    h, e = halves.shape[1:]
    rows = sum(o.shape[0] for o in outs)
    cols = w_ref.shape[2]
    for g in range(3):
        for c in range(0, cols, tn):
            x = halves[start : start + rows // h].reshape(rows, e)
            acc = jnp.dot(x, w_ref[g, :, c : c + tn], preferred_element_type=F32)
            at = 0
            for o in outs:
                o[:, g * cols + c : g * cols + c + tn] = acc[at : at + o.shape[0]].astype(o.dtype)
                at += o.shape[0]


def project(order, mine, other, w, shape, kept):
    ys, xs = shape
    n, e = mine[0].shape
    h = n // 2
    cols = w.shape[2]
    sent = [ys] * (xs - 1) + [xs] * (ys - 1)
    shapes = [((k * h, 3 * cols), F32 if kept else BF16) for k in ([ys, xs] if kept else sent)]
    scratch = [pltpu.VMEM((2 * xs * ys, h, e), BF16)]
    kernel = functools.partial(project_kernel, min(cols, 256), shape, sum(sent) if kept else 0)
    outs = order.call(kernel, [*mine, *other, w], shapes, "keep" if kept else "send", scratch, shown=LONG if kept else 0)
    if kept:
        return outs
    got_a = [shift_rows(s, shape, 0, -dx) for dx, s in enumerate(outs[: xs - 1], 1)]
    got_c = [shift_rows(s, shape, -dy, 0) for dy, s in enumerate(outs[xs - 1 :], 1)]
    return got_a, got_c


def middle_kernel(count_a, count_c, *refs):
    keep_a, got_a = refs[0], refs[1 : 1 + count_a]
    keep_c, got_c = refs[1 + count_a], refs[2 + count_a : 2 + count_a + count_c]
    outs = refs[2 + count_a + count_c :]
    h = outs[0].shape[0]
    for keep, got, mids in ((keep_a, got_a, outs[:count_c]), (keep_c, got_c, outs[count_c:])):
        for i, mid in enumerate(mids, 1):
            total = keep[i * h : (i + 1) * h]
            for g in got:
                total = total + g[i * h : (i + 1) * h].astype(F32)
            mid[...] = total.astype(BF16)


def middle(order, terms, h, shape):
    ys, xs = shape
    first, second = terms
    n = first[0].shape[1]
    mids = order.call(
        functools.partial(middle_kernel, xs - 1, ys - 1), [*first, *second], [((h, n), BF16)] * (xs + ys - 2), "middle"
    )
    last_a = [shift_rows(s, shape, -dy, 0) for dy, s in enumerate(mids[: ys - 1], 1)]
    last_c = [shift_rows(s, shape, 0, -dx) for dx, s in enumerate(mids[ys - 1 :], 1)]
    return [*first, *last_a], [*second, *last_c]


def finish_kernel(top, bottom, n, count_a, count_c, dones, *refs):
    refs = list(refs)
    terms = [refs[:count_a], refs[count_a : count_a + count_c]]
    del refs[: count_a + count_c]
    fin, fmix = refs.pop(0), refs.pop(0)
    follow = refs.pop(0) if not bottom else None
    rim = refs.pop(0) if top else None
    done = [refs.pop(0) for _ in range(dones)]
    out = refs.pop(0)
    lead = refs.pop(0) if not top else None
    tail = refs.pop(0) if bottom else None
    copies = []
    if top:
        whole, out, sems = out, refs.pop(), refs.pop()
        row = whole.shape[0]
        for i, o in enumerate([*done, out]):
            row -= o.shape[0]
            copies.append(pltpu.make_async_copy(o, whole.at[pl.ds(row, o.shape[0])], sems.at[i]))
        for c in copies[:-1]:
            c.start()
    ext, prod = refs
    h = n // 2
    for i, group in enumerate(terms):
        total = group[0][:h]
        for g in group[1:]:
            total = total + g[:h].astype(F32)
        ext[RIM + i * h : RIM + (i + 1) * h] = total
    if follow is not None:
        ext[RIM + n : RIM + n + RIM] = follow[...]
    if rim is not None:
        ext[:RIM] = rim[...].astype(F32)
    if lead is not None:
        lead[...] = ext[RIM : 2 * RIM]
    if tail is not None:
        tail[...] = ext[n : n + RIM].astype(BF16)
    cols = fmix.shape[1]
    first = RIM if top else 2 * RIM
    rows = out.shape[0]
    step = max(s for s in range(16, STEP + 1, 8) if rows % s == 0)

    def column(c, _):
        at = pl.multiple_of(c * LANES, LANES)

        def conv(g, start, count):
            where = pl.ds(pl.multiple_of(g * cols + at, LANES), LANES)
            total = fin[g, 0:1, pl.ds(at, LANES)] * ext[start : start + count, where]
            for s in range(1, 7):
                total = total + fin[g, s : s + 1, pl.ds(at, LANES)] * ext[start - s : start - s + count, where]
            return total

        for r in range(0, rows, step):
            base = first + r
            prod[: step + 8] = conv(1, base - 8, step + 8) * conv(2, base - 8, step + 8)
            mix = fmix[0:1, pl.ds(at, LANES)] * prod[8 : 8 + step]
            for s in range(1, 7):
                mix = mix + fmix[s : s + 1, pl.ds(at, LANES)] * prod[8 - s : 8 - s + step]
            out[r : r + step, pl.ds(at, LANES)] = (conv(0, base, step) * mix).astype(BF16)
        return 0

    lax.fori_loop(0, cols // LANES, column, 0)
    for c in copies[-1:]:
        c.start()
    for c in copies:
        c.wait()


def finish(order, top, bottom, n, terms, fin, fmix, follow, rim, done):
    width = terms[0][0].shape[1]
    cols = fmix.shape[1]
    rows = n + (RIM if top else 0) - (RIM if bottom else 0)
    args = [*terms[0], *terms[1], fin, fmix]
    args += [follow] if not bottom else []
    args += [rim, *done] if top else []
    height = rows + sum(o.shape[0] for o in done)
    shapes = [((height if top else rows, cols), BF16)]
    shapes += [((RIM, width), F32)] if not top else []
    shapes += [((RIM, width), BF16)] if bottom else []
    kernel = functools.partial(finish_kernel, top, bottom, n, len(terms[0]), len(terms[1]), len(done) if top else 0)
    scratch = [pltpu.VMEM((n + 2 * RIM, width), F32), pltpu.VMEM((STEP + 8, LANES), F32)]
    scratch += [pltpu.SemaphoreType.DMA((len(done) + 1,)), pltpu.VMEM((rows, cols), BF16)] if top else []
    return order.call(kernel, args, shapes, "finish", scratch, shown=LONG if bottom else 0, last=top)


CHUNKS = ((3,), (3, 2))
PLAN = ("W", "K0", "C0", "J0", "B0", "K1", "C1", "C2", "M0", "Y2", "J1", "B1", "F0", "J2", "B2", "M1", "M2", "F1", "F2")


def per_device(tokens, w_in, filt_in, filt_mix):
    rows = tokens.shape[0]
    cols = lax.axis_size("col")
    count = lax.axis_size("row")
    shape = side(count)
    order = Order()
    fin = filt_in.transpose(1, 0, 2)
    swap = [(c, c ^ 1) for c in range(cols)]
    parts = [[rows * k // 8 for k in chunk] for chunk in CHUNKS]
    sizes = sum(parts, [])
    last = len(sizes) - 1
    wide = widen(order, tokens, lax.ppermute(tokens, "col", swap), [sum(p) for p in parts])
    blocks = [gather(piece) for piece in wide]
    mine, outs, other, got, terms = [], [], {}, {}, {}
    follow, rim = None, None
    for step in PLAN:
        kind, i = step[0], int(step[1:] or 0)
        if kind == "W":
            w = fetch(order, w_in)
        elif kind == "Y":
            order.wait += other[i]
        elif kind == "K":
            mine += cut(order, blocks[i], parts[i])
        elif kind == "C":
            other[i] = [lax.ppermute(b, "col", swap) for b in mine[i]]
        elif kind == "J":
            got[i] = project(order, mine[i], other[i], w, shape, False)
        elif kind == "B":
            keep = project(order, mine[i], other[i], w, shape, True)
            terms[i] = [[k, *g] for k, g in zip(keep, got[i])]
        elif kind == "M":
            terms[i] = middle(order, terms[i], sizes[i] // 2, shape)
        else:
            made = finish(order, i == last, i == 0, sizes[i], terms[i], fin, filt_mix, follow, rim, outs)
            outs.append(made.pop(0))
            if i < last:
                follow = made.pop(0)
            if i == 0:
                rim = lax.ppermute(made.pop(0), "row", [(r, r + 1) for r in range(count - 1)])
    return outs[-1]


def solution(mesh):
    return jax.shard_map(
        per_device,
        mesh=mesh,
        in_specs=(P("row", "col"), P("row", None, "col"), P(None, None, "col"), P(None, "col")),
        out_specs=P("row", "col"),
        check_vma=False,
    )
```

```python
import functools

import jax
import jax.numpy as jnp
from jax import lax
from jax.experimental import pallas as pl
from jax.experimental.pallas import tpu as pltpu
from jax.sharding import PartitionSpec as P

CORES = 2
RIM = 16
STEP = 72
LANES = 128
LONG = 10 * 10**9
VMEM = pl.BlockSpec(memory_space=pltpu.VMEM)
HBM = pl.BlockSpec(memory_space=pl.ANY)
BF16, F32 = jnp.bfloat16, jnp.float32


def params(mib=16):
    return pltpu.CompilerParams(vmem_limit_bytes=mib * 2**20)


class Order:
    def __init__(self):
        self.last = None
        self.wait = []

    def call(self, kernel, args, shapes, name, scratch=(), specs=None, shown=0, last=False):
        specs = [VMEM] * len(args) if specs is None else specs
        extra = [*([] if self.last is None else [self.last]), *self.wait]
        self.wait = []
        count = len(args)

        def body(*refs):
            kernel(*refs[:count], *refs[count + len(extra) :])

        outs = pl.pallas_call(
            body,
            in_specs=specs + [HBM] * len(extra),
            out_specs=[HBM if last else VMEM] * len(shapes),
            out_shape=[jax.ShapeDtypeStruct(s, t) if last else pltpu.VMEM(s, t) for s, t in shapes],
            scratch_shapes=list(scratch),
            compiler_params=params(),
            cost_estimate=pl.CostEstimate(flops=shown, bytes_accessed=0, transcendentals=0),
            name=name,
        )(*args, *extra)
        self.last = outs[-1]
        return list(outs)


def side(n):
    x = 1
    while x * x < n:
        x *= 2
    return n // x, x


def shift_rows(block, shape, dy, dx):
    ys, xs = shape
    route = []
    for y in range(ys):
        for x in range(xs):
            route.append((((y + dy) % ys) * xs + (x + dx) % xs, y * xs + x))
    return lax.ppermute(block, "row", route)


def widen_kernel(own, other, *refs):
    *outs, sems = refs
    e = own.shape[1]
    core = lax.rem(lax.axis_index("col"), CORES)
    for k in range(CORES):

        @pl.when(core == k)
        def _():
            copies = []
            row = own.shape[0]
            for i, o in enumerate(outs):
                row -= o.shape[0]
                source = own.at[pl.ds(row, o.shape[0])]
                copies.append(pltpu.make_async_copy(source, o.at[:, pl.ds(k * e, e)], sems.at[i]))
            for c in copies:
                c.start()
            row = own.shape[0]
            for o in outs:
                row -= o.shape[0]
                o[:, (1 - k) * e : (2 - k) * e] = other[row : row + o.shape[0]]
            for c in copies:
                c.wait()


def widen(order, own, other, sizes):
    shapes = [((n, CORES * own.shape[1]), BF16) for n in sizes]
    own = pltpu.with_memory_space_constraint(own, pltpu.HBM)
    scratch = [pltpu.SemaphoreType.DMA((len(sizes),))]
    return order.call(widen_kernel, [own, other], shapes, "widen", scratch, specs=[HBM, VMEM])


def gather(piece):
    count, cols = lax.axis_size("row"), lax.axis_size("col")
    planes = cols // CORES
    assert count == planes and count & (count - 1) == 0

    def place(row, plane, core):
        return row * cols + plane * CORES + core

    blocks = []
    for a in reversed(range(count // CORES)):
        route = []
        for row in range(count):
            for plane in range(planes):
                for core in range(CORES):
                    route.append((place(row, plane, core), place(plane, row ^ (core * (count // CORES) + a), core)))
        blocks.append(lax.ppermute(piece, ("row", "col"), route))
    return blocks[::-1]


def cut_kernel(sizes, count, *refs):
    outs = iter(refs[count:])
    for block in refs[:count]:
        end = block.shape[0]
        for n in sizes:
            next(outs)[...] = block[end - n : end]
            end -= n


def cut(order, blocks, sizes):
    e = blocks[0].shape[1]
    kernel = functools.partial(cut_kernel, sizes, len(blocks))
    outs = order.call(kernel, blocks, [((n, e), BF16) for _ in blocks for n in sizes], "cut")
    return [outs[i :: len(sizes)] for i in range(len(sizes))]


def stack_halves(shape, mine, other, out):
    ys, xs = shape
    h = out.shape[1]
    me = lax.axis_index("row")
    plane = lax.axis_index("col") // CORES
    core = lax.rem(lax.axis_index("col"), CORES)
    sent = (xs - 1) * ys + (ys - 1) * xs
    for a in range(len(mine)):
        for blocks, j in ((mine, core * len(mine) + a), (other, (1 - core) * len(mine) + a)):
            row = lax.bitwise_xor(plane, j)
            dy = lax.rem(row // xs - me // xs + ys, ys)
            dx = lax.rem(lax.rem(row, xs) - lax.rem(me, xs) + xs, xs)
            out[jnp.where(dx > 0, (dx - 1) * ys + dy, sent + dy)] = blocks[a][:h]
            out[jnp.where(dy > 0, (xs - 1) * ys + (dy - 1) * xs + dx, sent + ys + dx)] = blocks[a][h:]


def fetch_kernel(w_ref, o_ref, sems):
    copies = [pltpu.make_async_copy(w_ref.at[g], o_ref.at[g], sems.at[g]) for g in range(3)]
    for c in copies:
        c.start()
    for c in copies:
        c.wait()


def fetch(order, w_in):
    w = pltpu.with_memory_space_constraint(w_in.transpose(1, 0, 2), pltpu.HBM)
    scratch = [pltpu.SemaphoreType.DMA((3,))]
    return order.call(fetch_kernel, [w], [(w.shape, BF16)], "fetch_w", scratch, specs=[HBM])[0]


def project_kernel(tn, shape, start, *refs):
    count = shape[0] * shape[1] // CORES
    mine, other, w_ref = refs[:count], refs[count : 2 * count], refs[2 * count]
    *outs, halves = refs[2 * count + 1 :]
    stack_halves(shape, mine, other, halves)
    h, e = halves.shape[1:]
    rows = sum(o.shape[0] for o in outs)
    cols = w_ref.shape[2]
    for g in range(3):
        for c in range(0, cols, tn):
            x = halves[start : start + rows // h].reshape(rows, e)
            acc = jnp.dot(x, w_ref[g, :, c : c + tn], preferred_element_type=F32)
            at = 0
            for o in outs:
                o[:, g * cols + c : g * cols + c + tn] = acc[at : at + o.shape[0]].astype(o.dtype)
                at += o.shape[0]


def project(order, mine, other, w, shape, kept):
    ys, xs = shape
    n, e = mine[0].shape
    h = n // 2
    cols = w.shape[2]
    sent = [ys] * (xs - 1) + [xs] * (ys - 1)
    shapes = [((k * h, 3 * cols), F32 if kept else BF16) for k in ([ys, xs] if kept else sent)]
    scratch = [pltpu.VMEM((2 * xs * ys, h, e), BF16)]
    kernel = functools.partial(project_kernel, min(cols, 256), shape, sum(sent) if kept else 0)
    outs = order.call(kernel, [*mine, *other, w], shapes, "keep" if kept else "send", scratch, shown=LONG if kept else 0)
    if kept:
        return outs
    got_a = [shift_rows(s, shape, 0, -dx) for dx, s in enumerate(outs[: xs - 1], 1)]
    got_c = [shift_rows(s, shape, -dy, 0) for dy, s in enumerate(outs[xs - 1 :], 1)]
    return got_a, got_c


def middle_kernel(count_a, count_c, *refs):
    keep_a, got_a = refs[0], refs[1 : 1 + count_a]
    keep_c, got_c = refs[1 + count_a], refs[2 + count_a : 2 + count_a + count_c]
    outs = refs[2 + count_a + count_c :]
    h = outs[0].shape[0]
    for keep, got, mids in ((keep_a, got_a, outs[:count_c]), (keep_c, got_c, outs[count_c:])):
        for i, mid in enumerate(mids, 1):
            total = keep[i * h : (i + 1) * h]
            for g in got:
                total = total + g[i * h : (i + 1) * h].astype(F32)
            mid[...] = total.astype(BF16)


def middle(order, terms, h, shape):
    ys, xs = shape
    first, second = terms
    n = first[0].shape[1]
    mids = order.call(
        functools.partial(middle_kernel, xs - 1, ys - 1), [*first, *second], [((h, n), BF16)] * (xs + ys - 2), "middle"
    )
    last_a = [shift_rows(s, shape, -dy, 0) for dy, s in enumerate(mids[: ys - 1], 1)]
    last_c = [shift_rows(s, shape, 0, -dx) for dx, s in enumerate(mids[ys - 1 :], 1)]
    return [*first, *last_a], [*second, *last_c]


def finish_kernel(top, bottom, n, count_a, count_c, dones, *refs):
    refs = list(refs)
    terms = [refs[:count_a], refs[count_a : count_a + count_c]]
    del refs[: count_a + count_c]
    fin, fmix = refs.pop(0), refs.pop(0)
    follow = refs.pop(0) if not bottom else None
    rim = refs.pop(0) if top else None
    done = [refs.pop(0) for _ in range(dones)]
    out = refs.pop(0)
    lead = refs.pop(0) if not top else None
    tail = refs.pop(0) if bottom else None
    copies = []
    if top:
        whole, out, sems = out, refs.pop(), refs.pop()
        row = whole.shape[0]
        for i, o in enumerate([*done, out]):
            row -= o.shape[0]
            copies.append(pltpu.make_async_copy(o, whole.at[pl.ds(row, o.shape[0])], sems.at[i]))
        for c in copies[:-1]:
            c.start()
    ext, prod = refs
    h = n // 2
    for i, group in enumerate(terms):
        total = group[0][:h]
        for g in group[1:]:
            total = total + g[:h].astype(F32)
        ext[RIM + i * h : RIM + (i + 1) * h] = total
    if follow is not None:
        ext[RIM + n : RIM + n + RIM] = follow[...]
    if rim is not None:
        ext[:RIM] = rim[...].astype(F32)
    if lead is not None:
        lead[...] = ext[RIM : 2 * RIM]
    if tail is not None:
        tail[...] = ext[n : n + RIM].astype(BF16)
    cols = fmix.shape[1]
    first = RIM if top else 2 * RIM
    rows = out.shape[0]
    step = max(s for s in range(16, STEP + 1, 8) if rows % s == 0)

    def column(c, _):
        at = pl.multiple_of(c * LANES, LANES)

        def conv(g, start, count):
            where = pl.ds(pl.multiple_of(g * cols + at, LANES), LANES)
            total = fin[g, 0:1, pl.ds(at, LANES)] * ext[start : start + count, where]
            for s in range(1, 7):
                total = total + fin[g, s : s + 1, pl.ds(at, LANES)] * ext[start - s : start - s + count, where]
            return total

        for r in range(0, rows, step):
            base = first + r
            prod[: step + 8] = conv(1, base - 8, step + 8) * conv(2, base - 8, step + 8)
            mix = fmix[0:1, pl.ds(at, LANES)] * prod[8 : 8 + step]
            for s in range(1, 7):
                mix = mix + fmix[s : s + 1, pl.ds(at, LANES)] * prod[8 - s : 8 - s + step]
            out[r : r + step, pl.ds(at, LANES)] = (conv(0, base, step) * mix).astype(BF16)
        return 0

    lax.fori_loop(0, cols // LANES, column, 0)
    for c in copies[-1:]:
        c.start()
    for c in copies:
        c.wait()


def finish(order, top, bottom, n, terms, fin, fmix, follow, rim, done):
    width = terms[0][0].shape[1]
    cols = fmix.shape[1]
    rows = n + (RIM if top else 0) - (RIM if bottom else 0)
    args = [*terms[0], *terms[1], fin, fmix]
    args += [follow] if not bottom else []
    args += [rim, *done] if top else []
    height = rows + sum(o.shape[0] for o in done)
    shapes = [((height if top else rows, cols), BF16)]
    shapes += [((RIM, width), F32)] if not top else []
    shapes += [((RIM, width), BF16)] if bottom else []
    kernel = functools.partial(finish_kernel, top, bottom, n, len(terms[0]), len(terms[1]), len(done) if top else 0)
    scratch = [pltpu.VMEM((n + 2 * RIM, width), F32), pltpu.VMEM((STEP + 8, LANES), F32)]
    scratch += [pltpu.SemaphoreType.DMA((len(done) + 1,)), pltpu.VMEM((rows, cols), BF16)] if top else []
    return order.call(kernel, args, shapes, "finish", scratch, shown=LONG if bottom else 0, last=top)


CHUNKS = ((3,), (3, 2))
PLAN = ("W", "K0", "C0", "J0", "B0", "K1", "C1", "C2", "M0", "Y2", "J1", "B1", "F0", "J2", "B2", "M1", "M2", "F1", "F2")


def per_device(tokens, w_in, filt_in, filt_mix):
    rows = tokens.shape[0]
    cols = lax.axis_size("col")
    count = lax.axis_size("row")
    shape = side(count)
    order = Order()
    fin = filt_in.transpose(1, 0, 2)
    swap = [(c, c ^ 1) for c in range(cols)]
    parts = [[rows * k // 8 for k in chunk] for chunk in CHUNKS]
    sizes = sum(parts, [])
    last = len(sizes) - 1
    wide = widen(order, tokens, lax.ppermute(tokens, "col", swap), [sum(p) for p in parts])
    blocks = [gather(piece) for piece in wide]
    mine, outs, other, got, terms = [], [], {}, {}, {}
    follow, rim = None, None
    for step in PLAN:
        kind, i = step[0], int(step[1:] or 0)
        if kind == "W":
            w = fetch(order, w_in)
        elif kind == "Y":
            order.wait += other[i]
        elif kind == "K":
            mine += cut(order, blocks[i], parts[i])
        elif kind == "C":
            other[i] = [lax.ppermute(b, "col", swap) for b in mine[i]]
        elif kind == "J":
            got[i] = project(order, mine[i], other[i], w, shape, False)
        elif kind == "B":
            keep = project(order, mine[i], other[i], w, shape, True)
            terms[i] = [[k, *g] for k, g in zip(keep, got[i])]
        elif kind == "M":
            terms[i] = middle(order, terms[i], sizes[i] // 2, shape)
        else:
            made = finish(order, i == last, i == 0, sizes[i], terms[i], fin, filt_mix, follow, rim, outs)
            outs.append(made.pop(0))
            if i < last:
                follow = made.pop(0)
            if i == 0:
                rim = lax.ppermute(made.pop(0), "row", [(r, r + 1) for r in range(count - 1)])
    return outs[-1]


def solution(mesh):
    return jax.shard_map(
        per_device,
        mesh=mesh,
        in_specs=(P("row", "col"), P("row", None, "col"), P(None, None, "col"), P(None, "col")),
        out_specs=P("row", "col"),
        check_vma=False,
    )
```
